32 devices in a mesh: lang: 4 (over x, core), blk: 8 (over z, y).
Axes of the slice: x: 2, y: 2, z: 4, core: 2. Of those that a mesh axis runs over, the one named last changes fastest.
Arguments:
- fisher: bfloat16 [8, 4096, 16384], P('lang', None, 'blk'), may hold values from 0.049804688 to 5
- factor_left: bfloat16 [8, 4096, 64], P('lang', 'blk'), may hold values from -6 to 6
- factor_right: bfloat16 [8, 64, 16384], P('lang', None, 'blk'), may hold values from -0.75 to 0.75
- base_weight: bfloat16 [4096, 16384], P(('lang', 'blk')), may hold values from -3 to 3
Outputs:
- merged: bfloat16 [4096, 16384], P(('lang', 'blk'))
The draws below stay inside these ranges and needn't reach their ends.
All inputs are finite; a program needn't handle non-finite values.
Results may differ from the reference program's by a relative error of at most 0.0011.
Values may be sent and summed in bfloat16 or wider, within the bound.
No kernel may reach another device: no remote copies, remote signals or barrier semaphores. Data moves between devices by JAX's collectives and lax.ppermute only.
A program may use at most 256 MiB of HBM per device.

```python
import math
import jax
import jax.numpy as jnp
from jax import lax

D = 4096
FFW = 16384
R = 64
LANGS = 8


def shard_levels(key, extent, split, low, top_value):
    def one(position, parts):
        steps = jax.random.uniform(jax.random.fold_in(jax.random.fold_in(key, 6), position), (parts,), jnp.float32, low / len(split), top_value / len(split))
        return jnp.repeat(jnp.exp(steps), extent[position] // parts).reshape((-1,) + (1,) * (len(extent) - position - 1))

    level = one(*split[0])
    for cut in split[1:]:
        level = level * one(*cut)
    return level


def noise(key, shape, scale, limit, split=(), kind=jnp.bfloat16):
    factor_of = shard_levels(key, shape, split, -0.22, 0.18) if split else 1.0
    values = jax.random.normal(key, shape, jnp.float32) * scale * factor_of
    return jnp.minimum(jnp.maximum(values, -limit), limit).astype(kind)


def setup_inputs(seed: int = 0) -> dict:
    key_list = jax.random.split(jax.random.key(seed), 5)
    return {
        "fisher": jnp.clip(jnp.exp(math.log(5.0) - 4.609084 * jax.random.uniform(key_list[0], (LANGS, D, FFW), jnp.float32) ** shard_levels(key_list[0], (LANGS, D, FFW), ((0, 4), (2, 8)), -0.2, 0.2)), 0.049804688, 5.0).astype(jnp.bfloat16),
        "factor_left": noise(key_list[1], (LANGS, D, R), 1.0, 6.0, ((0, 4), (1, 8))),
        "factor_right": noise(key_list[2], (LANGS, R, FFW), R ** -0.5, 0.75, ((0, 4), (2, 8))),
        "base_weight": noise(key_list[3], (D, FFW), 0.5, 3.0, ((0, 32),)),
    }


def reference(fisher, factor_left, factor_right, base_weight):
    def add_language(carry, inputs):
        weighted, totals = carry
        weight, left, right = inputs
        change = jnp.dot(left, right, preferred_element_type=jnp.float32)
        weight_wide = weight.astype(jnp.float32)
        return (weighted + weight_wide * change, totals + weight_wide), None

    zeros = jnp.zeros(base_weight.shape, jnp.float32)
    (weighted, totals), _ = lax.scan(add_language, (zeros, zeros), (fisher, factor_left, factor_right))
    return (base_weight.astype(jnp.float32) + weighted / totals).astype(jnp.bfloat16)
```

```python
import functools

import jax
import jax.numpy as jnp
from jax import lax
from jax.experimental import pallas as pl
from jax.experimental.pallas import tpu as pltpu
from jax.sharding import PartitionSpec as P

F32 = jnp.float32
BF16 = jnp.bfloat16
TINY = 2.0**-126
LAG = 4
VMEM = 64 * 1024 * 1024 - 128 * 1024


def encode_total(t):
    t = t * 0.5
    for _ in range(5):
        t = t * t
    return t.astype(BF16)


def decode_total(code):
    t = code.astype(F32)
    for _ in range(4):
        t = lax.rsqrt(t)
    return 2.0 * t * lax.rsqrt(t)


def encode_signed(v):
    v2 = v * v
    v4 = v2 * v2
    return (v4 * v2 * (v * jnp.abs(v))).astype(BF16)


def decode_signed(code):
    code = code.astype(F32)
    a = lax.rsqrt(jnp.maximum(jnp.abs(code), TINY))
    d = lax.rsqrt(lax.rsqrt(a))
    return code * a * (d * d * d)


def sum_totals(fishers):
    total = None
    for ref in fishers:
        for lang in range(ref.shape[0]):
            wide = ref[lang].astype(F32)
            total = wide if total is None else total + wide
    return total


def sum_weighted(fishers, lefts, rights):
    weighted = None
    for ref, left, right in zip(fishers, lefts, rights):
        rank = right.shape[1]
        for lang in range(ref.shape[0]):
            change = jnp.dot(left[:, lang * rank : (lang + 1) * rank], right[lang], preferred_element_type=F32)
            term = ref[lang].astype(F32) * change
            weighted = term if weighted is None else weighted + term
    return weighted


def sum_all(fishers, lefts, rights):
    totals, weighted = None, None
    for ref, left, right in zip(fishers, lefts, rights):
        rank = right.shape[1]
        for lang in range(ref.shape[0]):
            change = jnp.dot(left[:, lang * rank : (lang + 1) * rank], right[lang], preferred_element_type=F32)
            wide = ref[lang].astype(F32)
            totals = wide if totals is None else totals + wide
            weighted = wide * change if weighted is None else weighted + wide * change
    return totals, weighted


def copy_body(src, out):
    out[...] = src[...]


def totals_body(own, peer, out):
    out[...] = encode_total(sum_totals((own, peer)))


def weighted_body(own, peer, left_own, left_peer, right_own, right_peer, out):
    _, weighted = sum_all((own, peer), (left_own, left_peer), (right_own, right_peer))
    out[...] = encode_signed(weighted)


def both_body(own, peer, left_own, left_peer, right_own, right_peer, out_totals, out_weighted):
    totals, weighted = sum_all((own, peer), (left_own, left_peer), (right_own, right_peer))
    out_totals[...] = encode_total(totals)
    out_weighted[...] = encode_signed(weighted)


def ratio(own, peer, left_own, left_peer, right_own, right_peer, total_code, weighted_code):
    totals, weighted = sum_all((own, peer), (left_own, left_peer), (right_own, right_peer))
    return (weighted + decode_signed(weighted_code[...])) / (totals + decode_total(total_code[...]))


def ratio_body(*refs):
    refs[-1][...] = encode_signed(ratio(*refs[:8]))


def merge_own_body(*refs):
    refs[-1][...] = (refs[8][...].astype(F32) + ratio(*refs[:8])).astype(BF16)


def merge_body(code, base, out):
    out[...] = (base[...].astype(F32) + decode_signed(code[...])).astype(BF16)


def merge_many_body(*refs):
    *codes, base, out = refs
    for i, code in enumerate(codes):

        @pl.when(pl.program_id(0) == i)
        def _():
            merge_body(code, base, out)


def run_parts(parts, skipped, place, *refs):
    taken = sum(count for _, count, _ in parts)
    ins, outs = refs[:taken], refs[taken + skipped :]
    for body, count, results in parts:
        body(*ins[:count], *outs[:results])
        ins, outs = ins[count:], outs[results:]


def shards(fisher, factor_left, factor_right, base_weight):
    lang_count = lax.axis_size("lang")
    blk_count = lax.axis_size("blk")
    langs, full_rows, cols = fisher.shape
    rows = base_weight.shape[0]
    rank = factor_right.shape[1]
    steps = 8
    group = blk_count // steps
    band = group * rows
    tile = min(1024, cols)
    tiles = cols // tile
    half = lang_count // 2
    sides = half

    lang, blk = lax.axis_index("lang"), lax.axis_index("blk")
    core, side = lax.rem(lang, 2), lax.div(lang, 2)
    high = lax.div(blk, group)

    def over_core(a):
        return lax.ppermute(a, "lang", [(i, i ^ 1) for i in range(lang_count)])

    def over_x(a):
        return lax.ppermute(a, "lang", [(i, i ^ half) for i in range(lang_count)])

    bands = fisher.reshape(langs, lang_count * steps, band, cols)
    by_owner = fisher.reshape(langs, sides, 2 * steps, band, cols)

    ANY = pl.BlockSpec(memory_space=pl.ANY)
    last = [None]

    def call(parts, deps=(), alias=None, grid=(tiles,)):
        counts = [(body, len(operands), len(shapes)) for body, operands, _, shapes, _ in parts]
        operands, specs, shapes, out_specs = ([one for part in parts for one in part[k]] for k in range(1, 5))
        deps = list(deps) + ([last[0]] if last[0] is not None and last[0] is not alias else [])
        tail = deps + ([alias] if alias is not None else [])
        results = pl.pallas_call(
            functools.partial(run_parts, counts, len(tail)),
            out_shape=shapes,
            grid_spec=pltpu.PrefetchScalarGridSpec(
                num_scalar_prefetch=1,
                grid=grid,
                in_specs=specs + [ANY] * len(tail),
                out_specs=out_specs,
            ),
            input_output_aliases={} if alias is None else {len(operands) + len(tail): 0},
            compiler_params=pltpu.CompilerParams(vmem_limit_bytes=VMEM),
        )(place, *operands, *tail)
        last[0] = results[0]
        return list(results)

    place = jnp.stack([high, core, side, blk]).astype(jnp.int32)

    def owner(s, far, step):
        at_side = 1 - s[2] if far else s[2]
        return (at_side * 2 + s[1]) * steps + lax.bitwise_xor(s[0], step)

    right_peer = over_core(factor_right)
    left = factor_left.transpose(1, 0, 2).reshape(-1, langs * rank)
    shard_rows = left.shape[0]
    rounds = []
    relative = shard_rows % band == 0
    if relative:
        bit = blk_count // 2
        while bit:
            left = jnp.concatenate([left, lax.ppermute(left, "blk", [(i, i ^ bit) for i in range(blk_count)])])
            rounds.append(left)
            bit //= 2
    else:
        left = lax.all_gather(left, "blk", axis=0, tiled=True)
    left_peer = over_core(left).reshape(-1, band, langs * rank)
    left_bands = left.reshape(-1, band, langs * rank)

    def left_band(s, far, step):
        index = owner(s, far, step)
        if not relative:
            return index
        inside = shard_rows // band
        apart = lax.bitwise_xor(lax.div(index, inside), s[3])
        shard, bit = 0, blk_count // 2
        while bit:
            shard, apart, bit = shard + lax.rem(apart, 2) * bit, lax.div(apart, 2), bit // 2
        return shard * inside + lax.rem(index, inside)

    factors = (left_bands, left_peer, factor_right, right_peer)

    code_shape = jax.ShapeDtypeStruct((band, cols), BF16)
    out_shape = jax.ShapeDtypeStruct(base_weight.shape, BF16)

    right_spec = pl.BlockSpec((langs, rank, tile), lambda j, s: (0, 0, j))
    flat_spec = pl.BlockSpec((band, tile), lambda j, s: (0, j))

    def fisher_specs(far, step, whole):
        own = pl.BlockSpec((langs, None, band, tile), lambda j, s: (0, owner(s, far, step), 0, j))
        if whole:
            return own, pl.BlockSpec((langs, None, band, tile), lambda j, s: (0, 1 - s[2] if far else s[2], 0, j))
        return own, pl.BlockSpec((langs, None, band, tile), lambda j, s: (0, 0, 0, j))

    def factor_specs(far, step):
        return (
            pl.BlockSpec((None, band, langs * rank), lambda j, s: (left_band(s, far, step), 0, 0)),
            pl.BlockSpec((None, band, langs * rank), lambda j, s: (left_band(s, far, step), 0, 0)),
            right_spec,
            right_spec,
        )

    order = [7, 6, 5, 4, 3, 2, 1, 0]
    peers = {}
    arrived = {}
    crossed = []
    ratios = {}

    def copy_part(step, far=None):
        def other(s):
            return (1 - s[1]) * steps + lax.bitwise_xor(s[0], step)

        if far is None:
            src = pl.BlockSpec((langs, sides, None, band, tile), lambda j, s: (0, 0, other(s), 0, j))
            out = pl.BlockSpec((langs, sides, band, tile), lambda j, s: (0, 0, 0, j))
            shape = jax.ShapeDtypeStruct((langs, sides, band, cols), BF16)
        else:
            src = pl.BlockSpec((langs, 1, None, band, tile), lambda j, s: (0, 1 - s[2] if far else s[2], other(s), 0, j))
            out = pl.BlockSpec((langs, 1, band, tile), lambda j, s: (0, 0, 0, j))
            shape = jax.ShapeDtypeStruct((langs, 1, band, cols), BF16)
        return copy_body, (by_owner,), (src,), [shape], [out]

    def exchange(where, piece):
        step, far = (*where, None)[:2]
        piece = over_core(piece)
        for which in (True, False) if far is None else (far,):
            peers[step, which] = (piece, far is None)

    def send_part(body, step):
        peer, whole = peers[step, True]
        operands, specs = (bands, peer), fisher_specs(True, step, whole)
        if body is not totals_body:
            operands, specs = operands + factors, specs + factor_specs(True, step)
        codes = 2 if body is both_body else 1
        return body, operands, specs, [code_shape] * codes, [flat_spec] * codes

    def near_operands(step):
        peer, whole = peers[step, False]
        return (bands, peer, *factors, *arrived[step]), (*fisher_specs(False, step, whole), *factor_specs(False, step), flat_spec, flat_spec)

    def divide_part(step):
        return ratio_body, *near_operands(step), [code_shape], [flat_spec]

    def to_owner(step, code):
        if step:
            code = lax.ppermute(code, "blk", [(i, i ^ (step * group)) for i in range(blk_count)])
        if group > 1:
            near_groups = [[h * group + g for g in range(group)] for h in range(steps)]
            code = lax.all_to_all(code.reshape(group, rows, cols), "blk", 0, 0, axis_index_groups=near_groups, tiled=True)
        ratios[step] = code.reshape(group, rows, cols)

    def stage(send=None, copies=(), divide=None, deps=()):
        parts = []
        if send is not None:
            parts.append(send_part(*send))
        for copy in copies:
            parts.append(copy_part(*copy))
        if divide is not None:
            parts.append(divide_part(divide))
        late = list(ratios.values())[-LAG:][:1] if len(ratios) >= LAG else []
        results = call(parts, deps=list(deps) + (crossed[-2] if len(crossed) > 1 else []) + late)
        if send is not None:
            body, step = send
            codes, results = results[: len(parts[0][3])], results[len(parts[0][3]) :]
            crossed.append([over_x(code) for code in codes])
            arrived.setdefault(step, []).extend(crossed[-1])
        for copy in copies:
            exchange(copy, results.pop(0))
        if divide is not None:
            to_owner(divide, results.pop(0))

    a = order
    stage(copies=[(a[0], True)])
    stage(copies=[(a[1],), (a[2],)])
    stage((totals_body, a[0]), copies=[(a[3],), (a[0], False)], deps=rounds[:1])
    stage((totals_body, a[1]), copies=[(a[4],)])
    stage((totals_body, a[2]), copies=[(a[5],)], deps=rounds[1:2])
    stage((totals_body, a[3]), copies=[(a[6],)])
    stage((totals_body, a[4]), copies=[(a[7],)], deps=rounds[2:])
    stage((weighted_body, a[0]))
    stage((weighted_body, a[1]))
    stage((weighted_body, a[2]), divide=a[0])
    stage((weighted_body, a[3]), divide=a[1])
    stage((weighted_body, a[4]), divide=a[2])
    stage((both_body, a[5]), divide=a[3])
    stage((both_body, a[6]), divide=a[4])
    stage((both_body, a[7]), divide=a[5])
    stage(divide=a[6])
    merged = None

    def merge(done):
        nonlocal merged
        for part in range(group):

            def column(i, s, part=part):
                step = done[0]
                for n in range(1, len(done)):
                    step = jnp.where(i == n, done[n], step)
                return (0, lax.bitwise_xor(s[0], step) * group + part)

            code_spec = pl.BlockSpec((None, rows, cols), lambda i, s, part=part: (part, 0, 0))
            column_spec = pl.BlockSpec((rows, cols), column)
            merged = call(
                [(merge_many_body, (*(ratios[step] for step in done), base_weight), (code_spec,) * len(done) + (column_spec,), [out_shape], [column_spec])],
                alias=merged,
                grid=(len(done),),
            )[0]

    merge(a[:4])
    merge(a[4:6])
    if group == 1:
        merge(a[6:7])
        operands, specs = near_operands(a[7])
        column_spec = pl.BlockSpec((rows, tile), lambda j, s: (0, lax.bitwise_xor(s[0], a[7]) * tiles + j))
        merged = call([(merge_own_body, (*operands, base_weight), (*specs, column_spec), [out_shape], [column_spec])], alias=merged)[0]
    else:
        stage(divide=a[7])
        merge(a[6:])
    return merged


def solution(mesh):
    placed = (
        P("lang", None, "blk"),
        P("lang", "blk", None),
        P("lang", None, "blk"),
        P(("lang", "blk"), None),
    )
    return jax.shard_map(
        shards, mesh=mesh, in_specs=placed, out_specs=P(("lang", "blk"), None), check_vma=False
    )
```

```python
import functools

import jax
import jax.numpy as jnp
from jax import lax
from jax.experimental import pallas as pl
from jax.experimental.pallas import tpu as pltpu
from jax.sharding import PartitionSpec as P

F32 = jnp.float32
BF16 = jnp.bfloat16
TINY = 2.0**-126
UP_WEIGHTED = 2.0**3
UP_RATIO = 2.0**7
WINDOW = 3
LAG = 3
VMEM = 64 * 1024 * 1024 - 128 * 1024


def encode_total(t):
    t = t * 0.5
    for _ in range(5):
        t = t * t
    return t.astype(BF16)


def decode_total(code):
    t = code.astype(F32)
    for _ in range(4):
        t = lax.rsqrt(t)
    return 2.0 * t * lax.rsqrt(t)


def encode_signed(v, up):
    v = v * up
    v2 = v * v
    v4 = v2 * v2
    return (v4 * v2 * (v * jnp.abs(v))).astype(BF16)


def decode_signed(code, up):
    code = code.astype(F32)
    a = lax.rsqrt(jnp.maximum(jnp.abs(code), TINY))
    d = lax.rsqrt(lax.rsqrt(a))
    return code * a * (d * d * d) * (1.0 / up)


def sum_totals(fishers):
    total = None
    for ref in fishers:
        for lang in range(ref.shape[0]):
            wide = ref[lang].astype(F32)
            total = wide if total is None else total + wide
    return total


def sum_weighted(fishers, lefts, rights):
    weighted = None
    for ref, left, right in zip(fishers, lefts, rights):
        rank = right.shape[1]
        for lang in range(ref.shape[0]):
            change = jnp.dot(left[:, lang * rank : (lang + 1) * rank], right[lang], preferred_element_type=F32)
            term = ref[lang].astype(F32) * change
            weighted = term if weighted is None else weighted + term
    return weighted


def sum_all(place, half, own, peer, *factors):
    if half is None:
        left_own, left_peer, right_own, right_peer, *rest = factors
        lefts = (left_own[...], left_peer[...])
    else:
        own_low, own_high, peer_low, peer_high, right_own, right_peer, *rest = factors
        high = half(place) == 1
        lefts = (jnp.where(high, own_high[...], own_low[...]), jnp.where(high, peer_high[...], peer_low[...]))
    totals, weighted = None, None
    for ref, left, right in zip((own, peer), lefts, (right_own, right_peer)):
        rank = right.shape[1]
        for lang in range(ref.shape[0]):
            change = jnp.dot(left[:, lang * rank : (lang + 1) * rank], right[lang], preferred_element_type=F32)
            wide = ref[lang].astype(F32)
            totals = wide if totals is None else totals + wide
            weighted = wide * change if weighted is None else weighted + wide * change
    return totals, weighted, rest


def copy_body(pieces, steps, place, src, out, held, into, outof):
    high, core, side = place[0], place[1], place[2]
    copies = []
    for i, (step, far) in enumerate(pieces):
        band = (1 - core) * steps + lax.bitwise_xor(high, step)
        for lang in range(src.shape[0]):
            rows = src.at[lang, 1 - side if far else side, band]
            first = pltpu.make_async_copy(rows, held.at[i, lang], into.at[i, lang])
            first.start()
            copies.append((first, pltpu.make_async_copy(held.at[i, lang], out.at[i, lang], outof.at[i, lang])))
    for first, second in copies:
        first.wait()
        second.start()
    for _, second in copies:
        second.wait()


def join_body(place, first, second, out):
    count = first.shape[0]
    out[:count] = first[...]
    out[count:] = second[...]


def totals_body(place, own, peer, out):
    out[...] = encode_total(sum_totals((own, peer)))


def many_totals_body(place, *refs):
    out = refs[-1]
    for i in range(out.shape[0]):
        out[i] = encode_total(sum_totals(refs[2 * i : 2 * i + 2]))


def weighted_body(half, place, *refs):
    _, weighted, (out,) = sum_all(place, half, *refs)
    out[...] = encode_signed(weighted, UP_WEIGHTED)


def ratio(half, place, *refs):
    totals, weighted, (total_code, weighted_code, *rest) = sum_all(place, half, *refs)
    return (weighted + decode_signed(weighted_code[...], UP_WEIGHTED)) / (totals + decode_total(total_code[...])), rest


def ratio_body(half, place, *refs):
    value, (out,) = ratio(half, place, *refs)
    out[...] = encode_signed(value, UP_RATIO)


def merge_own_body(half, place, *refs):
    value, (base, out) = ratio(half, place, *refs)
    out[...] = (base[...].astype(F32) + value).astype(BF16)


def merge_body(place, code, base, out):
    out[...] = (base[...].astype(F32) + decode_signed(code[...], UP_RATIO)).astype(BF16)


def merge_many_body(place, *refs):
    *codes, base, out = refs
    for i, code in enumerate(codes):

        @pl.when(pl.program_id(0) == i)
        def _():
            merge_body(place, code, base, out)


def run_parts(parts, skipped, scratch, place, *refs):
    taken = sum(count for _, count, _ in parts)
    ins, outs, own = refs[:taken], refs[taken + skipped : len(refs) - scratch], refs[len(refs) - scratch :]
    for body, count, results in parts:
        body(place, *ins[:count], *outs[:results], *own)
        ins, outs = ins[count:], outs[results:]


def shards(fisher, factor_left, factor_right, base_weight):
    lang_count = lax.axis_size("lang")
    blk_count = lax.axis_size("blk")
    langs, full_rows, cols = fisher.shape
    rows = base_weight.shape[0]
    rank = factor_right.shape[1]
    steps = 8
    group = blk_count // steps
    band = group * rows
    tile = min(1024, cols)
    tiles = cols // tile
    half = lang_count // 2
    sides = half

    lang, blk = lax.axis_index("lang"), lax.axis_index("blk")
    core, side = lax.rem(lang, 2), lax.div(lang, 2)
    high = lax.div(blk, group)

    def over_core(a):
        return lax.ppermute(a, "lang", [(i, i ^ 1) for i in range(lang_count)])

    def over_x(a):
        return lax.ppermute(a, "lang", [(i, i ^ half) for i in range(lang_count)])

    bands = fisher.reshape(langs, lang_count * steps, band, cols)
    by_owner = fisher.reshape(langs, sides, 2 * steps, band, cols)

    ANY = pl.BlockSpec(memory_space=pl.ANY)
    last = [None]

    def call(parts, deps=(), alias=None, grid=(tiles,), scratch=()):
        counts = [(body, len(operands), len(shapes)) for body, operands, _, shapes, _ in parts]
        operands, specs, shapes, out_specs = ([one for part in parts for one in part[k]] for k in range(1, 5))
        deps = list(deps) + ([last[0]] if last[0] is not None and last[0] is not alias else [])
        tail = deps + ([alias] if alias is not None else [])
        results = pl.pallas_call(
            functools.partial(run_parts, counts, len(tail), len(scratch)),
            out_shape=shapes,
            grid_spec=pltpu.PrefetchScalarGridSpec(
                num_scalar_prefetch=1,
                grid=grid,
                in_specs=specs + [ANY] * len(tail),
                out_specs=out_specs,
                scratch_shapes=list(scratch),
            ),
            input_output_aliases={} if alias is None else {len(operands) + len(tail): 0},
            compiler_params=pltpu.CompilerParams(vmem_limit_bytes=VMEM),
        )(place, *operands, *tail)
        last[0] = results[0]
        return list(results)

    place = jnp.stack([high, core, side, blk]).astype(jnp.int32)

    def owner(s, far, step):
        at_side = 1 - s[2] if far else s[2]
        return (at_side * 2 + s[1]) * steps + lax.bitwise_xor(s[0], step)

    right_peer = over_core(factor_right)
    left = factor_left.transpose(1, 0, 2).reshape(-1, langs * rank)
    shard_rows = left.shape[0]
    rounds = []
    relative = shard_rows % band == 0
    if relative:
        bit = blk_count // 2
        while bit:
            rounds.append(bit)
            bit //= 2
    else:
        left = lax.all_gather(left, "blk", axis=0, tiled=True)

    inside = max(shard_rows // band, 1)

    def apart(s, far, step):
        return lax.bitwise_xor(lax.div(owner(s, far, step), inside), s[3])

    def left_band(s, far, step):
        if not relative:
            return owner(s, far, step)
        rest, shard, bit = lax.div(apart(s, far, step), 2), 0, blk_count // 4
        while bit:
            shard, rest, bit = shard + lax.rem(rest, 2) * bit, lax.div(rest, 2), bit // 2
        return shard * inside + lax.rem(owner(s, far, step), inside)

    def which_half(far, step):
        if not relative:
            return None
        return lambda s: lax.rem(apart(s, far, step), 2)

    factors = []

    def has_left(parts):
        factors[:] = [part.reshape(-1, band, langs * rank) for part in (*parts, *map(over_core, parts))] + [factor_right, right_peer]

    if not relative:
        has_left([left])

    code_shape = jax.ShapeDtypeStruct((band, cols), BF16)
    out_shape = jax.ShapeDtypeStruct(base_weight.shape, BF16)

    right_spec = pl.BlockSpec((langs, rank, tile), lambda j, s: (0, 0, j))
    flat_spec = pl.BlockSpec((band, tile), lambda j, s: (0, j))

    def fisher_specs(far, step, piece):
        return (
            pl.BlockSpec((langs, None, band, tile), lambda j, s: (0, owner(s, far, step), 0, j)),
            pl.BlockSpec((None, langs, band, tile), lambda j, s: (piece, 0, 0, j)),
        )

    def factor_specs(far, step):
        return (
            *[pl.BlockSpec((None, band, langs * rank), lambda j, s: (left_band(s, far, step), 0, 0))] * (len(factors) - 2),
            right_spec,
            right_spec,
        )

    order = [7, 3, 6, 2, 5, 4, 1, 0]
    peers = {}
    arrived = {}
    crossed = []
    ratios = {}
    to_come = []

    def exchange(pieces, deps=()):
        count = len(pieces)
        scratch = [pltpu.VMEM((count, langs, band, cols), BF16)] + [pltpu.SemaphoreType.DMA((count, langs))] * 2
        shape = jax.ShapeDtypeStruct((count, langs, band, cols), BF16)
        out = call(
            [(functools.partial(copy_body, pieces, steps), (by_owner,), (ANY,), [shape], [ANY])],
            deps=deps,
            grid=(1,),
            scratch=scratch,
        )[0]
        out = over_core(out)
        for i, (step, far) in enumerate(pieces):
            peers[step, bool(far)] = (out, i)
        return out

    def send_part(body, step):
        peer, piece = peers[step, True]
        operands, specs = (bands, peer), fisher_specs(True, step, piece)
        if body is weighted_body:
            body = functools.partial(body, which_half(True, step))
            operands, specs = operands + tuple(factors), specs + factor_specs(True, step)
        return body, operands, specs, [code_shape], [flat_spec]

    def near_operands(step):
        peer, piece = peers[step, False]
        codes, specs = zip(*arrived[step])
        return (bands, peer, *factors, *codes), (*fisher_specs(False, step, piece), *factor_specs(False, step), *specs)

    def many_totals_part(those):
        operands, specs = [], []
        for step in those:
            peer, piece = peers[step, True]
            operands += [bands, peer]
            specs += fisher_specs(True, step, piece)
        shape = jax.ShapeDtypeStruct((len(those), band, cols), BF16)
        return many_totals_body, operands, specs, [shape], [pl.BlockSpec((len(those), band, tile), lambda j, s: (0, 0, j))]

    def divide_part(step):
        return functools.partial(ratio_body, which_half(False, step)), *near_operands(step), [code_shape], [flat_spec]

    def to_owner(step, code):
        if step:
            code = lax.ppermute(code, "blk", [(i, i ^ (step * group)) for i in range(blk_count)])
        if group > 1:
            near_groups = [[h * group + g for g in range(group)] for h in range(steps)]
            code = lax.all_to_all(code.reshape(group, rows, cols), "blk", 0, 0, axis_index_groups=near_groups, tiled=True)
        ratios[step] = code.reshape(group, rows, cols)

    def left_round():
        nonlocal left_from
        bit = rounds[joined]
        left_from = lax.ppermute(left, "blk", [(i, i ^ bit) for i in range(blk_count)])

    def join_part():
        count, width = left.shape
        half_spec = pl.BlockSpec((count, width), lambda j, s: (0, 0))
        whole_spec = pl.BlockSpec((2 * count, width), lambda j, s: (0, 0))
        return join_body, (left, left_from), (half_spec, half_spec), [jax.ShapeDtypeStruct((2 * count, width), BF16)], [whole_spec]

    left_from, joined = None, 0
    if relative:
        left_round()

    def stage(send=None, divide=None, deps=(), join=False):
        nonlocal left, joined
        join = join and relative
        parts = []
        if send is not None:
            parts.append(many_totals_part(send[1]) if isinstance(send[1], list) else send_part(*send))
        if divide is not None:
            parts.append(divide_part(divide))
        if join:
            parts.append(join_part())
        if not parts:
            return
        late = [code for at, code in to_come if at <= len(crossed) - LAG]
        to_come[:] = [(at, code) for at, code in to_come if at > len(crossed) - LAG]
        results = call(parts, deps=list(deps) + (crossed[-WINDOW:][:1] if len(crossed) >= WINDOW else []) + late)
        if send is not None:
            crossed.append(over_x(results.pop(0)))
            if isinstance(send[1], list):
                for i, step in enumerate(send[1]):
                    arrived[step] = [(crossed[-1], pl.BlockSpec((None, band, tile), lambda j, s, i=i: (i, 0, j)))]
            else:
                arrived.setdefault(send[1], []).append((crossed[-1], flat_spec))
        if divide is not None:
            to_owner(divide, results.pop(0))
            to_come.append((len(crossed) - 1, ratios[divide]))
        if join:
            left, joined = results.pop(0), joined + 1
            left_round()
            if joined == len(rounds) - 1:
                has_left([left, left_from])

    a = order
    first = exchange([(step, 1) for step in a[:4]])
    exchange([(step, 0) for step in a[:4]] + [(step, far) for step in a[4:] for far in (1, 0)], deps=[first, right_peer] + ([left_from] if relative else []))
    stage((totals_body, a[:4]), join=True)
    stage(join=True)
    stage((weighted_body, a[0]))
    stage((weighted_body, a[1]))
    stage((weighted_body, a[2]))
    stage((weighted_body, a[3]), divide=a[0])
    stage((totals_body, a[4]), divide=a[1])
    stage((weighted_body, a[4]), divide=a[2])
    stage((totals_body, a[5]), divide=a[3])
    stage((weighted_body, a[5]))
    stage((totals_body, a[6]), divide=a[4])
    stage((weighted_body, a[6]))
    stage((totals_body, a[7]), divide=a[5])
    stage((weighted_body, a[7]))
    stage(divide=a[6])
    merged = None

    def merge(done):
        nonlocal merged
        for part in range(group):

            def column(i, s, part=part):
                step = done[0]
                for n in range(1, len(done)):
                    step = jnp.where(i == n, done[n], step)
                return (0, lax.bitwise_xor(s[0], step) * group + part)

            code_spec = pl.BlockSpec((None, rows, cols), lambda i, s, part=part: (part, 0, 0))
            column_spec = pl.BlockSpec((rows, cols), column)
            merged = call(
                [(merge_many_body, (*(ratios[step] for step in done), base_weight), (code_spec,) * len(done) + (column_spec,), [out_shape], [column_spec])],
                alias=merged,
                grid=(len(done),),
            )[0]

    merge(a[:4])
    merge(a[4:6])
    if group == 1:
        merge(a[6:7])
        operands, specs = near_operands(a[7])
        column_spec = pl.BlockSpec((rows, tile), lambda j, s: (0, lax.bitwise_xor(s[0], a[7]) * tiles + j))
        merged = call([(functools.partial(merge_own_body, which_half(False, a[7])), (*operands, base_weight), (*specs, column_spec), [out_shape], [column_spec])], alias=merged)[0]
    else:
        stage(divide=a[7])
        merge(a[6:])
    return merged


def solution(mesh):
    placed = (
        P("lang", None, "blk"),
        P("lang", "blk", None),
        P("lang", None, "blk"),
        P(("lang", "blk"), None),
    )
    return jax.shard_map(
        shards, mesh=mesh, in_specs=placed, out_specs=P(("lang", "blk"), None), check_vma=False
    )
```
